32 devices in a mesh: grp: 4 (over x, core), wide: 8 (over z, y).
Axes of the slice: x: 2, y: 2, z: 4, core: 2. Of those that a mesh axis runs over, the one named last changes fastest.
Arguments:
- anchor_states: bfloat16 [4096, 1024], P(('wide', 'grp')), may hold values from -6 to 6
- key_weight: bfloat16 [1024, 1024], P(None, 'grp'), may hold values from -0.1875 to 0.1875
- value_weight: bfloat16 [1024, 1024], P(None, 'grp'), may hold values from -0.1875 to 0.1875
- panel_query: bfloat16 [8192, 1024], P(('wide', 'grp')), may hold values from -160 to 160
- cell_list: int32 [64, 4], P('wide'), may hold values from 0 to 3, as said below
- cell_count: int32 [64], P('wide'), may hold values from 1 to 4, as said below
- norm_gain: float32 [1024], replicated, may hold values from 0.1 to 1.9
- up_weight: bfloat16 [1024, 512], replicated, may hold values from -0.1875 to 0.1875
- flux_weight: bfloat16 [4, 512], replicated, may hold values from -0.25 to 0.25
Outputs:
- flux: float32 [4, 8192], P(None, ('wide', 'grp'))
The draws below stay inside these ranges and needn't reach their ends.
Inputs may be any that keep to these rules, and one draw needn't show every extreme that they name: `cell_list`: the entries of a row are distinct cell blocks of that panel block's region; entries past cell_count are not used. `cell_count`: every region has a panel block whose list uses all 4 slots.
All inputs are finite; a program needn't handle non-finite values.
Results may differ from the reference program's by a relative error of at most 0.007.
Values may be sent and summed in bfloat16 or wider, within the bound.
A program may use at most 64 MiB of HBM per device.

```python
import math
import jax
import jax.numpy as jnp
from jax import lax

D = 1024
HEADS = 16
FF = 512
NF = 4
BLK = 128
LMAX = 4
HD = 64
ANCHORS = 4096
PANELS = 8192
REGION_ANCHORS = 512
REGION_PANELS = 1024
SLAB = 128
REGION_BLOCKS = 8
CBLK = 4
NBLK = 64
N_WIDE = 8


def draw_cell_list(key, part):
    scores = jax.random.randint(key, (NBLK, CBLK), 0, 1 << 20) * CBLK + jnp.arange(CBLK, dtype=jnp.int32)[None, :]
    order = jnp.argsort(scores, axis=1)
    return order[:, :LMAX].astype(jnp.int32)


def draw_cell_count(key, part):
    per_region = NBLK // N_WIDE
    base = jax.random.randint(jax.random.fold_in(key, 1), (NBLK,), 1, LMAX + 1)
    pick = jax.random.randint(jax.random.fold_in(key, 2), (N_WIDE,), 0, per_region)
    rows = jnp.arange(NBLK, dtype=jnp.int32)
    chosen = rows % per_region == pick[rows // per_region]
    return jnp.where(chosen, LMAX, base).astype(jnp.int32)


def draw_panel_query(key, part):
    row_scale = jnp.exp(jax.random.uniform(jax.random.fold_in(key, 3), (PANELS, 1), minval=math.log(0.3), maxval=math.log(3.0)))
    base = jnp.clip(jax.random.normal(jax.random.fold_in(key, 4), (PANELS, D)), -6.0, 6.0)
    scale = row_scale
    return (base * scale).astype(jnp.bfloat16)


def block_scale(key, dims, split, smallest, high):
    def one(dim, parts):
        draws = jax.random.uniform(jax.random.fold_in(jax.random.fold_in(key, 6), dim), (parts,), jnp.float32, smallest / len(split), high / len(split))
        return jnp.repeat(jnp.exp(draws), dims[dim] // parts).reshape((-1,) + (1,) * (len(dims) - dim - 1))

    factor_of = one(*split[0])
    for cut in split[1:]:
        factor_of = factor_of * one(*cut)
    return factor_of


def normal_values(key, extent, deviation, most, cuts=(), held_as=jnp.bfloat16):
    values = deviation * jax.random.normal(key, extent, jnp.float32)
    if cuts:
        values = values * block_scale(key, extent, cuts, -0.22, 0.18)
    return jnp.clip(values, -most, most).astype(held_as)


def setup_inputs(seed: int = 0) -> dict:
    key_of = jax.random.split(jax.random.key(seed), 10)
    return {
        "anchor_states": normal_values(key_of[0], (ANCHORS, D), 1.0, 6.0, ((0, 32),)),
        "key_weight": normal_values(key_of[1], (D, D), D ** -0.5, 0.1875, ((1, 4),)),
        "value_weight": normal_values(key_of[2], (D, D), D ** -0.5, 0.1875, ((1, 4),)),
        "panel_query": draw_panel_query(jax.random.fold_in(key_of[9], 71), 0),
        "cell_list": draw_cell_list(jax.random.fold_in(key_of[9], 71), 0),
        "cell_count": draw_cell_count(jax.random.fold_in(key_of[9], 71), 0),
        "norm_gain": jnp.clip(1.0 + 0.18 * jax.random.normal(key_of[6], (D,), jnp.float32), 0.1, 1.9),
        "up_weight": normal_values(key_of[7], (D, FF), D ** -0.5, 0.1875),
        "flux_weight": normal_values(key_of[8], (NF, FF), FF ** -0.5, 0.25),
    }


def attend_region(region_keys, region_values, region_query, lists, counts):
    key_blocks = region_keys.reshape(CBLK, BLK, HEADS, HD)
    value_blocks = region_values.reshape(CBLK, BLK, HEADS, HD)
    query_blocks = region_query.reshape(REGION_BLOCKS, BLK, HEADS, HD)

    def one_block(item):
        query_block, listed, count = item
        picked_keys = key_blocks[listed].reshape(LMAX * BLK, HEADS, HD).astype(jnp.float32)
        picked_values = value_blocks[listed].reshape(LMAX * BLK, HEADS, HD).astype(jnp.float32)
        scores = jnp.einsum('ihd,jhd->hij', query_block.astype(jnp.float32), picked_keys) / math.sqrt(HD)
        valid = jnp.repeat(jnp.arange(LMAX, dtype=jnp.int32) < count, BLK)
        scores = jnp.where(valid[None, None, :], scores, -jnp.inf)
        top = lax.optimization_barrier(jnp.max(scores, axis=-1, keepdims=True))
        expo = jnp.exp(scores - top)
        weights = (expo / lax.optimization_barrier(jnp.sum(expo, axis=-1, keepdims=True))).astype(jnp.bfloat16)
        output = jnp.einsum('hij,jhd->ihd', weights.astype(jnp.float32), picked_values)
        return output.reshape(BLK, D).astype(jnp.bfloat16)
    return lax.map(one_block, (query_blocks, lists, counts))

def reference(anchor_states, key_weight, value_weight, panel_query, cell_list, cell_count, norm_gain, up_weight, flux_weight):
    keys = jnp.dot(anchor_states, key_weight, preferred_element_type=jnp.float32).astype(jnp.bfloat16)
    anchor_values = jnp.dot(anchor_states, value_weight, preferred_element_type=jnp.float32).astype(jnp.bfloat16)
    region_keys = keys.reshape(N_WIDE, REGION_ANCHORS, D)
    region_values = anchor_values.reshape(N_WIDE, REGION_ANCHORS, D)
    region_query = panel_query.reshape(N_WIDE, N_WIDE, SLAB, D).transpose(1, 0, 2, 3).reshape(N_WIDE, REGION_PANELS, D)
    lists = cell_list.reshape(N_WIDE, REGION_BLOCKS, LMAX)
    counts = cell_count.reshape(N_WIDE, REGION_BLOCKS)

    def one_region(item):
        return attend_region(item[0], item[1], item[2], item[3], item[4])
    attended = lax.map(one_region, (region_keys, region_values, region_query, lists, counts))
    attended = attended.reshape(N_WIDE, N_WIDE, SLAB, D).transpose(1, 0, 2, 3).reshape(PANELS, D)
    stream = panel_query.astype(jnp.float32) + attended.astype(jnp.float32)
    scale = lax.rsqrt(lax.optimization_barrier(jnp.mean(stream * stream, axis=-1, keepdims=True)) + 1e-06)
    normed = (stream * scale * norm_gain.astype(jnp.float32)[None, :]).astype(jnp.bfloat16)
    hidden = jax.nn.gelu(jnp.dot(normed, up_weight, preferred_element_type=jnp.float32)).astype(jnp.bfloat16)
    flux = lax.dot_general(flux_weight, hidden, (((1,), (1,)), ((), ())), preferred_element_type=jnp.float32)
    return flux
```

```python
import functools
import math

import jax
import jax.numpy as jnp
from jax import lax
from jax.experimental import pallas as pl
from jax.experimental.pallas import tpu as pltpu
from jax.sharding import PartitionSpec as P

BLK = 128
LMAX = 4
HD = 64
LANES = 128
MESH = pl.DeviceIdType.MESH


def flip(index, bits):
    bit = 1
    while bit <= bits:
        if bits & bit:
            index = index + bit * (1 - 2 * ((index // bit) % 2))
        bit *= 2
    return index


def kernel(
    n_wide,
    n_grp,
    anchor_hbm,
    key_hbm,
    value_hbm,
    query_hbm,
    list_ref,
    count_ref,
    gain_ref,
    up_hbm,
    flux_w_ref,
    flux_ref,
    anchors,
    weights,
    keys,
    values,
    region_query,
    outgoing,
    attended,
    query,
    up,
    local_sem,
    anchor_send,
    anchor_recv,
    forward_send,
    query_send,
    query_recv,
    out_send,
    out_recv,
):
    w = lax.axis_index("wide")
    g = lax.axis_index("grp")
    slabs = n_wide // n_grp
    slab = region_query.shape[1]
    cols = region_query.shape[2]
    pairs = cols // LANES
    chips = n_grp // 2
    core = g % 2
    chip = g // 2
    sibling = chip * 2 + 1 - core
    home = w // slabs
    here = home == g

    loads = [
        pltpu.make_async_copy(anchor_hbm, anchors.at[g], local_sem.at[0]),
        pltpu.make_async_copy(key_hbm, weights.at[:, pl.ds(0, cols)], local_sem.at[1]),
        pltpu.make_async_copy(value_hbm, weights.at[:, pl.ds(cols, cols)], local_sem.at[2]),
        pltpu.make_async_copy(query_hbm, query, local_sem.at[3]),
        pltpu.make_async_copy(up_hbm, up, local_sem.at[4]),
    ]
    for load in loads:
        load.start()

    barrier = pltpu.get_barrier_semaphore()

    def greet(wide, grp):
        pl.semaphore_signal(barrier, inc=1, device_id=(grp, wide), device_id_type=MESH)

    @pl.loop(1, n_grp)
    def _(i):
        greet(w, (g + i) % n_grp)

    @pl.loop(0, n_wide)
    def _(i):
        region = g * slabs + i // n_grp
        head = i % n_grp

        @pl.when(jnp.logical_or(region != w, head != g))
        def _():
            greet(region, head)

        @pl.when(jnp.logical_or(i != w, home != g))
        def _():
            greet(i, home)

    pl.semaphore_wait(barrier, n_grp - 1 + 2 * n_wide - 2 * here.astype(jnp.int32))

    def anchor_copy(grp, index):
        return pltpu.make_async_remote_copy(
            src_ref=anchor_hbm,
            dst_ref=anchors.at[g],
            send_sem=anchor_send.at[index],
            recv_sem=anchor_recv.at[g],
            device_id=(grp, w),
            device_id_type=MESH,
        )

    for j in range(1, chips):
        anchor_copy(((chip + j) % chips) * 2 + core, j).start()
    anchor_copy(sibling, 0).start()

    def query_source(i):
        s = i // n_grp
        head = i % n_grp
        return query_hbm.at[
            pl.ds(pl.multiple_of(s * slab, 16), slab), pl.ds(pl.multiple_of(head * cols, LANES), cols)
        ]

    def query_copy(i):
        return pltpu.make_async_remote_copy(
            src_ref=query_source(i),
            dst_ref=region_query.at[w],
            send_sem=query_send.at[i],
            recv_sem=query_recv.at[w],
            device_id=(i % n_grp, g * slabs + i // n_grp),
            device_id_type=MESH,
        )

    def is_self(i):
        return jnp.logical_and(g * slabs + i // n_grp == w, i % n_grp == g)

    @pl.loop(0, n_wide)
    def _(i):
        @pl.when(is_self(i))
        def _():
            pltpu.make_async_copy(query_source(i), region_query.at[w], query_recv.at[w]).start()

        @pl.when(jnp.logical_not(is_self(i)))
        def _():
            query_copy(i).start()

    low = lax.broadcasted_iota(jnp.int32, (BLK, LANES), 1) < HD

    def project(cell):
        both = jnp.dot(anchors[cell], weights[...], preferred_element_type=jnp.float32)
        rows = pl.ds(pl.multiple_of(cell * BLK, BLK), BLK)
        for j in range(pairs):
            k = both[:, j * LANES : (j + 1) * LANES]
            v = both[:, cols + j * LANES : cols + (j + 1) * LANES]
            keys[j, 0, rows, :] = jnp.where(low, k, 0.0).astype(jnp.bfloat16)
            keys[j, 1, rows, :] = jnp.where(low, 0.0, k).astype(jnp.bfloat16)
            values[j, 0, rows, :] = jnp.where(low, v, 0.0).astype(jnp.bfloat16)
            values[j, 1, rows, :] = jnp.where(low, 0.0, v).astype(jnp.bfloat16)

    def wait_anchor(cell):
        pltpu.make_async_copy(anchors.at[cell], anchors.at[cell], anchor_recv.at[cell]).wait()

    def forward_copy(cell, j):
        return pltpu.make_async_remote_copy(
            src_ref=anchors.at[cell],
            dst_ref=anchors.at[cell],
            send_sem=forward_send.at[j],
            recv_sem=anchor_recv.at[cell],
            device_id=(sibling, w),
            device_id_type=MESH,
        )

    def across(j):
        return (chip + chips - j) % chips

    for load in loads[:3]:
        load.wait()
    project(g)
    wait_anchor(sibling)
    project(sibling)
    for j in range(1, chips):
        cell = across(j) * 2 + core
        wait_anchor(cell)
        forward_copy(cell, j).start()
        project(cell)
    for j in range(1, chips):
        cell = across(j) * 2 + 1 - core
        wait_anchor(cell)
        project(cell)

    scale = math.log2(math.e) / math.sqrt(HD)
    first = lax.broadcasted_iota(jnp.int32, (slab, LANES), 1) < HD
    nt = (((1,), (1,)), ((), ()))

    def out_copy(p):
        return pltpu.make_async_remote_copy(
            src_ref=outgoing.at[p],
            dst_ref=attended.at[g, w % slabs],
            send_sem=out_send.at[p],
            recv_sem=out_recv.at[g, w % slabs],
            device_id=(home, p),
            device_id_type=MESH,
        )

    def attend(p):
        block = p * slab // BLK
        used = count_ref[block]
        bias = []
        for c in range(n_grp):
            live = jnp.logical_and(list_ref[0, block] == c, used > 0)
            for slot in range(1, LMAX):
                live = jnp.logical_or(live, jnp.logical_and(list_ref[slot, block] == c, used > slot))
            bias.append(jnp.full((1, BLK), jnp.where(live, 0.0, -jnp.inf), jnp.float32))
        bias = jnp.concatenate(bias, axis=1)
        pltpu.make_async_copy(region_query.at[p], region_query.at[p], query_recv.at[p]).wait()
        for j in range(pairs):
            q = region_query[p, :, j * LANES : (j + 1) * LANES]
            total = None
            sums = []
            for i in range(2):
                scores = lax.dot_general(q, keys[j, i], nt, preferred_element_type=jnp.float32)
                scores = scores * scale + bias
                top = jnp.max(scores, axis=-1, keepdims=True)
                expo = jnp.exp2(scores - top)
                sums.append(jnp.sum(expo, axis=-1, keepdims=True))
                part = jnp.dot(
                    expo.astype(jnp.bfloat16), values[j, i], preferred_element_type=jnp.float32
                )
                total = part if total is None else total + part
            inverse = jnp.where(first, 1.0 / sums[0], 1.0 / sums[1])
            outgoing[p, :, j * LANES : (j + 1) * LANES] = (total * inverse).astype(jnp.bfloat16)

    @pl.loop(0, n_wide)
    def _(k):
        p = w
        bit = 1
        while bit < n_wide:
            step = (k // bit) % 2
            p = p + step * bit * (1 - 2 * ((p // bit) % 2))
            bit *= 2
        attend(p)
        mine = jnp.logical_and(p == w, here)

        @pl.when(mine)
        def _():
            pltpu.make_async_copy(
                outgoing.at[p], attended.at[g, w % slabs], out_recv.at[g, w % slabs]
            ).start()

        @pl.when(jnp.logical_not(mine))
        def _():
            out_copy(p).start()

    for load in loads[3:]:
        load.wait()
    for h in range(n_grp):
        for s in range(slabs):
            pltpu.make_async_copy(
                attended.at[h, s], attended.at[h, s], out_recv.at[h, s]
            ).wait()
    rows = query.shape[0]
    dim = query.shape[1]
    stream = []
    square = jnp.zeros((rows, 1), jnp.float32)
    for h in range(n_grp):
        part = query[:, h * cols : (h + 1) * cols].astype(jnp.float32) + attended[h].reshape(
            rows, cols
        ).astype(jnp.float32)
        square = square + jnp.sum(part * part, axis=-1, keepdims=True)
        stream.append(part)
    factor = lax.rsqrt(square / dim + 1e-06)
    normed = jnp.concatenate(
        [
            (stream[h] * factor * gain_ref[:, h * cols : (h + 1) * cols]).astype(jnp.bfloat16)
            for h in range(n_grp)
        ],
        axis=1,
    )
    hidden = jax.nn.gelu(
        jnp.dot(normed, up[...], preferred_element_type=jnp.float32), approximate=True
    ).astype(jnp.bfloat16)
    flux_ref[...] = lax.dot_general(flux_w_ref[...], hidden, nt, preferred_element_type=jnp.float32)

    for j in range(1, chips):
        anchor_copy(((chip + j) % chips) * 2 + core, j).wait_send()
        forward_copy(across(j) * 2 + core, j).wait_send()
    anchor_copy(sibling, 0).wait_send()

    @pl.loop(0, n_wide)
    def _(i):
        @pl.when(jnp.logical_not(is_self(i)))
        def _():
            query_copy(i).wait_send()

        @pl.when(jnp.logical_not(jnp.logical_and(i == w, here)))
        def _():
            out_copy(i).wait_send()


def body(n_wide, n_grp, anchor, key_w, value_w, query, cell_list, cell_count, gain, up, flux_w):
    rows, dim = query.shape
    cols = key_w.shape[1]
    slabs = n_wide // n_grp
    slab = rows // slabs
    cells = n_grp
    pairs = cols // LANES
    any_space = pl.BlockSpec(memory_space=pl.ANY)
    vmem = pl.BlockSpec(memory_space=pltpu.VMEM)
    smem = pl.BlockSpec(memory_space=pltpu.SMEM)
    bf16 = jnp.bfloat16
    dma = pltpu.SemaphoreType.DMA
    return pl.pallas_call(
        functools.partial(kernel, n_wide, n_grp),
        out_shape=jax.ShapeDtypeStruct((flux_w.shape[0], rows), jnp.float32),
        in_specs=[any_space] * 4 + [smem] * 2 + [vmem, any_space, vmem],
        out_specs=vmem,
        scratch_shapes=[
            pltpu.VMEM((cells, BLK, dim), bf16),
            pltpu.VMEM((dim, 2 * cols), bf16),
            pltpu.VMEM((pairs, 2, cells * BLK, LANES), bf16),
            pltpu.VMEM((pairs, 2, cells * BLK, LANES), bf16),
            pltpu.VMEM((n_wide, slab, cols), bf16),
            pltpu.VMEM((n_wide, slab, cols), bf16),
            pltpu.VMEM((n_grp, slabs, slab, cols), bf16),
            pltpu.VMEM((rows, dim), bf16),
            pltpu.VMEM(up.shape, bf16),
            dma((5,)),
            dma((max(n_grp // 2, 1),)),
            dma((n_grp,)),
            dma((max(n_grp // 2, 1),)),
            dma((n_wide,)),
            dma((n_wide,)),
            dma((n_wide,)),
            dma((n_grp, slabs)),
        ],
        compiler_params=pltpu.CompilerParams(
            collective_id=0, has_side_effects=True, vmem_limit_bytes=56 * 1024 * 1024
        ),
        cost_estimate=pl.CostEstimate(flops=3 * 10**9, bytes_accessed=6 * 10**6, transcendentals=0),
    )(anchor, key_w, value_w, query, cell_list.T, cell_count, gain[None, :], up, flux_w)


def solution(mesh):
    in_specs = (
        P(("wide", "grp"), None),
        P(None, "grp"),
        P(None, "grp"),
        P(("wide", "grp"), None),
        P("wide", None),
        P("wide"),
        P(),
        P(),
        P(),
    )
    out_specs = P(None, ("wide", "grp"))
    step = functools.partial(body, mesh.shape["wide"], mesh.shape["grp"])
    return jax.shard_map(step, mesh=mesh, in_specs=in_specs, out_specs=out_specs, check_vma=False)
```

```python
import functools
import math

import jax
import jax.numpy as jnp
from jax import lax
from jax.experimental import pallas as pl
from jax.experimental.pallas import tpu as pltpu
from jax.sharding import PartitionSpec as P

BLK = 128
LMAX = 4
HD = 64
LANES = 128
MESH = pl.DeviceIdType.MESH


def kernel(
    n_wide,
    n_grp,
    anchor_hbm,
    key_hbm,
    value_hbm,
    query_hbm,
    list_ref,
    count_ref,
    gain_ref,
    up_hbm,
    flux_w_ref,
    flux_ref,
    anchors,
    weights,
    keys,
    values,
    region_query,
    outgoing,
    attended,
    query,
    up,
    relay,
    back,
    local_sem,
    anchor_send,
    anchor_recv,
    forward_send,
    query_send,
    query_recv,
    out_send,
    out_recv,
    relay_send,
    relay_recv,
    back_send,
    back_recv,
):
    w = lax.axis_index("wide")
    g = lax.axis_index("grp")
    slabs = n_wide // n_grp
    slab = region_query.shape[1]
    cols = region_query.shape[2]
    pairs = cols // LANES
    chips = n_grp // 2
    core = g % 2
    chip = g // 2
    sibling = chip * 2 + 1 - core
    home = w // slabs
    here = home == g

    loads = [
        pltpu.make_async_copy(anchor_hbm, anchors.at[g], local_sem.at[0]),
        pltpu.make_async_copy(key_hbm, weights.at[:, pl.ds(0, cols)], local_sem.at[1]),
        pltpu.make_async_copy(value_hbm, weights.at[:, pl.ds(cols, cols)], local_sem.at[2]),
        pltpu.make_async_copy(query_hbm, query, local_sem.at[3]),
        pltpu.make_async_copy(up_hbm, up, local_sem.at[4]),
    ]
    for load in loads:
        load.start()

    barrier = pltpu.get_barrier_semaphore()

    def greet(wide, grp):
        pl.semaphore_signal(barrier, inc=1, device_id=(grp, wide), device_id_type=MESH)

    @pl.loop(1, n_grp)
    def _(i):
        greet(w, (g + i) % n_grp)

    @pl.loop(1, n_wide)
    def _(i):
        greet((w + i) % n_wide, g)
        greet((w + i) % n_wide, sibling)

    pl.semaphore_wait(barrier, n_grp - 1 + 2 * (n_wide - 1))

    def anchor_copy(grp, index):
        return pltpu.make_async_remote_copy(
            src_ref=anchor_hbm,
            dst_ref=anchors.at[g],
            send_sem=anchor_send.at[index],
            recv_sem=anchor_recv.at[g],
            device_id=(grp, w),
            device_id_type=MESH,
        )

    for j in range(1, chips):
        anchor_copy(((chip + j) % chips) * 2 + core, j).start()
    anchor_copy(sibling, 0).start()

    def query_source(s, head):
        return query_hbm.at[
            pl.ds(pl.multiple_of(s * slab, 16), slab), pl.ds(pl.multiple_of(head * cols, LANES), cols)
        ]

    def direct_copy(s, head):
        return pltpu.make_async_remote_copy(
            src_ref=query_source(s, head),
            dst_ref=region_query.at[w],
            send_sem=query_send.at[s * n_grp + head],
            recv_sem=query_recv.at[w],
            device_id=(head, g * slabs + s),
            device_id_type=MESH,
        )

    def relay_index(j, from_core, s):
        return ((j - 1) * 2 + from_core) * slabs + s

    def relayed_copy(j, s, head):
        index = relay_index(j, core, s)
        return pltpu.make_async_remote_copy(
            src_ref=query_source(s, head),
            dst_ref=relay.at[index],
            send_sem=query_send.at[s * n_grp + head],
            recv_sem=relay_recv.at[index],
            device_id=(head, w),
            device_id_type=MESH,
        )

    def each_query(act_relayed, act_direct, act_self):
        for j in range(1, chips):
            for c in range(2):
                head = ((chip + j) % chips) * 2 + c

                @pl.loop(0, slabs)
                def _(s):
                    same = g * slabs + s == w

                    @pl.when(same)
                    def _():
                        act_direct(s, head)

                    @pl.when(jnp.logical_not(same))
                    def _():
                        act_relayed(j, s, head)

        @pl.loop(0, slabs)
        def _(s):
            act_direct(s, sibling)
            same = g * slabs + s == w

            @pl.when(same)
            def _():
                act_self(s)

            @pl.when(jnp.logical_not(same))
            def _():
                act_direct(s, g)

    each_query(
        lambda j, s, head: relayed_copy(j, s, head).start(),
        lambda s, head: direct_copy(s, head).start(),
        lambda s: pltpu.make_async_copy(
            query_source(s, g), region_query.at[w], query_recv.at[w]
        ).start(),
    )

    def forward_query(j, c, s):
        index = relay_index(j, c, s)
        source = ((chip + chips - j) % chips) * 2 + c
        return pltpu.make_async_remote_copy(
            src_ref=relay.at[index],
            dst_ref=region_query.at[w],
            send_sem=relay_send.at[index],
            recv_sem=query_recv.at[w],
            device_id=(g, source * slabs + s),
            device_id_type=MESH,
        )

    def each_relay(act):
        for j in range(1, chips):
            for c in range(2):

                @pl.loop(0, slabs)
                def _(s):
                    source = ((chip + chips - j) % chips) * 2 + c

                    @pl.when(source * slabs + s != w)
                    def _():
                        act(j, c, s)

    low = lax.broadcasted_iota(jnp.int32, (BLK, LANES), 1) < HD

    def project(cell):
        both = jnp.dot(anchors[cell], weights[...], preferred_element_type=jnp.float32)
        rows = pl.ds(pl.multiple_of(cell * BLK, BLK), BLK)
        for j in range(pairs):
            k = both[:, j * LANES : (j + 1) * LANES]
            v = both[:, cols + j * LANES : cols + (j + 1) * LANES]
            keys[j, 0, rows, :] = jnp.where(low, k, 0.0).astype(jnp.bfloat16)
            keys[j, 1, rows, :] = jnp.where(low, 0.0, k).astype(jnp.bfloat16)
            values[j, 0, rows, :] = jnp.where(low, v, 0.0).astype(jnp.bfloat16)
            values[j, 1, rows, :] = jnp.where(low, 0.0, v).astype(jnp.bfloat16)

    def wait_anchor(cell):
        pltpu.make_async_copy(anchors.at[cell], anchors.at[cell], anchor_recv.at[cell]).wait()

    def forward_copy(cell, j):
        return pltpu.make_async_remote_copy(
            src_ref=anchors.at[cell],
            dst_ref=anchors.at[cell],
            send_sem=forward_send.at[j],
            recv_sem=anchor_recv.at[cell],
            device_id=(sibling, w),
            device_id_type=MESH,
        )

    def across(j):
        return (chip + chips - j) % chips

    for load in loads[:3]:
        load.wait()
    project(g)
    wait_anchor(sibling)
    project(sibling)
    for j in range(1, chips):
        cell = across(j) * 2 + core
        wait_anchor(cell)
        forward_copy(cell, j).start()
        project(cell)
    for j in range(1, chips):
        cell = across(j) * 2 + 1 - core
        wait_anchor(cell)
        project(cell)

    def pass_on(j, c, s):
        index = relay_index(j, c, s)
        pltpu.make_async_copy(relay.at[index], relay.at[index], relay_recv.at[index]).wait()
        forward_query(j, c, s).start()

    each_relay(pass_on)

    scale = math.log2(math.e) / math.sqrt(HD)
    first = lax.broadcasted_iota(jnp.int32, (slab, LANES), 1) < HD
    nt = (((1,), (1,)), ((), ()))

    def out_copy(p):
        return pltpu.make_async_remote_copy(
            src_ref=outgoing.at[p],
            dst_ref=attended.at[g, w % slabs],
            send_sem=out_send.at[p],
            recv_sem=out_recv.at[g, w % slabs],
            device_id=(home, p),
            device_id_type=MESH,
        )

    def hop_copy(p):
        return pltpu.make_async_remote_copy(
            src_ref=outgoing.at[p],
            dst_ref=back.at[w],
            send_sem=out_send.at[p],
            recv_sem=back_recv.at[w],
            device_id=(g, p),
            device_id_type=MESH,
        )

    def back_copy(r):
        return pltpu.make_async_remote_copy(
            src_ref=back.at[r],
            dst_ref=attended.at[g, r % slabs],
            send_sem=back_send.at[r],
            recv_sem=out_recv.at[g, r % slabs],
            device_id=(r // slabs, w),
            device_id_type=MESH,
        )

    def straight(p):
        return jnp.logical_or(home // 2 == chip, p == w)

    def flipped(k):
        p = w
        bit = 1
        while bit < n_wide:
            step = (k // bit) % 2
            p = p + step * bit * (1 - 2 * ((p // bit) % 2))
            bit *= 2
        return p

    def attend(p):
        block = p * slab // BLK
        used = count_ref[block]
        bias = []
        for c in range(n_grp):
            live = jnp.logical_and(list_ref[0, block] == c, used > 0)
            for slot in range(1, LMAX):
                live = jnp.logical_or(live, jnp.logical_and(list_ref[slot, block] == c, used > slot))
            bias.append(jnp.full((1, BLK), jnp.where(live, 0.0, -jnp.inf), jnp.float32))
        bias = jnp.concatenate(bias, axis=1)
        pltpu.make_async_copy(region_query.at[p], region_query.at[p], query_recv.at[p]).wait()
        for j in range(pairs):
            q = region_query[p, :, j * LANES : (j + 1) * LANES]
            total = None
            sums = []
            for i in range(2):
                scores = lax.dot_general(q, keys[j, i], nt, preferred_element_type=jnp.float32)
                scores = scores * scale + bias
                top = jnp.max(scores, axis=-1, keepdims=True)
                expo = jnp.exp2(scores - top)
                sums.append(jnp.sum(expo, axis=-1, keepdims=True))
                part = jnp.dot(
                    expo.astype(jnp.bfloat16), values[j, i], preferred_element_type=jnp.float32
                )
                total = part if total is None else total + part
            inverse = jnp.where(first, 1.0 / sums[0], 1.0 / sums[1])
            outgoing[p, :, j * LANES : (j + 1) * LANES] = (total * inverse).astype(jnp.bfloat16)

    @pl.loop(0, n_wide)
    def _(k):
        p = flipped(k)
        attend(p)
        mine = jnp.logical_and(p == w, here)

        @pl.when(mine)
        def _():
            pltpu.make_async_copy(
                outgoing.at[p], attended.at[g, w % slabs], out_recv.at[g, w % slabs]
            ).start()

        @pl.when(jnp.logical_and(straight(p), jnp.logical_not(mine)))
        def _():
            out_copy(p).start()

        @pl.when(jnp.logical_not(straight(p)))
        def _():
            hop_copy(p).start()

    @pl.loop(1, n_wide)
    def _(k):
        r = flipped(k)

        @pl.when((r // slabs) // 2 != chip)
        def _():
            pltpu.make_async_copy(back.at[r], back.at[r], back_recv.at[r]).wait()
            back_copy(r).start()

    for load in loads[3:]:
        load.wait()
    for h in range(n_grp):
        for s in range(slabs):
            pltpu.make_async_copy(
                attended.at[h, s], attended.at[h, s], out_recv.at[h, s]
            ).wait()
    rows = query.shape[0]
    dim = query.shape[1]
    stream = []
    square = jnp.zeros((rows, 1), jnp.float32)
    for h in range(n_grp):
        part = query[:, h * cols : (h + 1) * cols].astype(jnp.float32) + attended[h].reshape(
            rows, cols
        ).astype(jnp.float32)
        square = square + jnp.sum(part * part, axis=-1, keepdims=True)
        stream.append(part)
    factor = lax.rsqrt(square / dim + 1e-06)
    normed = jnp.concatenate(
        [
            (stream[h] * factor * gain_ref[:, h * cols : (h + 1) * cols]).astype(jnp.bfloat16)
            for h in range(n_grp)
        ],
        axis=1,
    )
    hidden = jax.nn.gelu(
        jnp.dot(normed, up[...], preferred_element_type=jnp.float32), approximate=True
    ).astype(jnp.bfloat16)
    flux_ref[...] = lax.dot_general(flux_w_ref[...], hidden, nt, preferred_element_type=jnp.float32)

    for j in range(1, chips):
        anchor_copy(((chip + j) % chips) * 2 + core, j).wait_send()
        forward_copy(across(j) * 2 + core, j).wait_send()
    anchor_copy(sibling, 0).wait_send()

    each_query(
        lambda j, s, head: relayed_copy(j, s, head).wait_send(),
        lambda s, head: direct_copy(s, head).wait_send(),
        lambda s: None,
    )
    each_relay(lambda j, c, s: forward_query(j, c, s).wait_send())

    @pl.loop(0, n_wide)
    def _(i):
        @pl.when(jnp.logical_not(jnp.logical_and(i == w, here)))
        def _():
            out_copy(i).wait_send()

        @pl.when(jnp.logical_and(i != w, (i // slabs) // 2 != chip))
        def _():
            back_copy(i).wait_send()


def body(n_wide, n_grp, anchor, key_w, value_w, query, cell_list, cell_count, gain, up, flux_w):
    rows, dim = query.shape
    cols = key_w.shape[1]
    slabs = n_wide // n_grp
    slab = rows // slabs
    cells = n_grp
    pairs = cols // LANES
    any_space = pl.BlockSpec(memory_space=pl.ANY)
    vmem = pl.BlockSpec(memory_space=pltpu.VMEM)
    smem = pl.BlockSpec(memory_space=pltpu.SMEM)
    bf16 = jnp.bfloat16
    dma = pltpu.SemaphoreType.DMA
    return pl.pallas_call(
        functools.partial(kernel, n_wide, n_grp),
        out_shape=jax.ShapeDtypeStruct((flux_w.shape[0], rows), jnp.float32),
        in_specs=[any_space] * 4 + [smem] * 2 + [vmem, any_space, vmem],
        out_specs=vmem,
        scratch_shapes=[
            pltpu.VMEM((cells, BLK, dim), bf16),
            pltpu.VMEM((dim, 2 * cols), bf16),
            pltpu.VMEM((pairs, 2, cells * BLK, LANES), bf16),
            pltpu.VMEM((pairs, 2, cells * BLK, LANES), bf16),
            pltpu.VMEM((n_wide, slab, cols), bf16),
            pltpu.VMEM((n_wide, slab, cols), bf16),
            pltpu.VMEM((n_grp, slabs, slab, cols), bf16),
            pltpu.VMEM((rows, dim), bf16),
            pltpu.VMEM(up.shape, bf16),
            pltpu.VMEM((max(n_grp - 2, 1) * slabs, slab, cols), bf16),
            pltpu.VMEM((n_wide, slab, cols), bf16),
            dma((5,)),
            dma((max(n_grp // 2, 1),)),
            dma((n_grp,)),
            dma((max(n_grp // 2, 1),)),
            dma((n_wide,)),
            dma((n_wide,)),
            dma((n_wide,)),
            dma((n_grp, slabs)),
            dma((max(n_grp - 2, 1) * slabs,)),
            dma((max(n_grp - 2, 1) * slabs,)),
            dma((n_wide,)),
            dma((n_wide,)),
        ],
        compiler_params=pltpu.CompilerParams(
            collective_id=0, has_side_effects=True, vmem_limit_bytes=56 * 1024 * 1024
        ),
        cost_estimate=pl.CostEstimate(flops=3 * 10**9, bytes_accessed=6 * 10**6, transcendentals=0),
    )(anchor, key_w, value_w, query, cell_list.T, cell_count, gain[None, :], up, flux_w)


def solution(mesh):
    in_specs = (
        P(("wide", "grp"), None),
        P(None, "grp"),
        P(None, "grp"),
        P(("wide", "grp"), None),
        P("wide", None),
        P("wide"),
        P(),
        P(),
        P(),
    )
    out_specs = P(None, ("wide", "grp"))
    step = functools.partial(body, mesh.shape["wide"], mesh.shape["grp"])
    return jax.shard_map(step, mesh=mesh, in_specs=in_specs, out_specs=out_specs, check_vma=False)
```

```python
import functools
import math

import jax
import jax.numpy as jnp
from jax import lax
from jax.experimental import pallas as pl
from jax.experimental.pallas import tpu as pltpu
from jax.sharding import PartitionSpec as P

BLK = 128
LMAX = 4
HD = 64
LANES = 128
ONES = 16
STEP = 256
MESH = pl.DeviceIdType.MESH


def kernel(
    n_wide,
    n_grp,
    anchor_hbm,
    key_hbm,
    value_hbm,
    query_hbm,
    list_ref,
    count_ref,
    gain_ref,
    up_hbm,
    flux_w_ref,
    flux_ref,
    anchors,
    weights,
    keys,
    values,
    region_query,
    outgoing,
    attended,
    query,
    up,
    local_sem,
    anchor_send,
    anchor_recv,
    forward_send,
    query_send,
    query_recv,
    out_send,
    out_recv,
):
    w = lax.axis_index("wide")
    g = lax.axis_index("grp")
    slabs = n_wide // n_grp
    slab = region_query.shape[1]
    cols = region_query.shape[2]
    pairs = cols // LANES
    chips = n_grp // 2
    core = g % 2
    chip = g // 2
    sibling = chip * 2 + 1 - core
    home = w // slabs
    here = home == g

    loads = [
        pltpu.make_async_copy(anchor_hbm, anchors.at[g], local_sem.at[0]),
        pltpu.make_async_copy(key_hbm, weights.at[:, pl.ds(0, cols)], local_sem.at[1]),
        pltpu.make_async_copy(value_hbm, weights.at[:, pl.ds(cols, cols)], local_sem.at[2]),
        pltpu.make_async_copy(query_hbm, query, local_sem.at[3]),
        pltpu.make_async_copy(up_hbm, up, local_sem.at[4]),
    ]
    for load in loads:
        load.start()

    barrier = pltpu.get_barrier_semaphore()

    def greet(wide, grp):
        pl.semaphore_signal(barrier, inc=1, device_id=(grp, wide), device_id_type=MESH)

    @pl.loop(1, n_grp)
    def _(i):
        greet(w, (g + i) % n_grp)

    @pl.loop(0, n_wide)
    def _(i):
        region = g * slabs + i // n_grp
        head = i % n_grp

        @pl.when(jnp.logical_or(region != w, head != g))
        def _():
            greet(region, head)

        @pl.when(jnp.logical_or(i != w, home != g))
        def _():
            greet(i, home)

    pl.semaphore_wait(barrier, n_grp - 1 + 2 * n_wide - 2 * here.astype(jnp.int32))

    def anchor_copy(grp, index):
        return pltpu.make_async_remote_copy(
            src_ref=anchor_hbm,
            dst_ref=anchors.at[g],
            send_sem=anchor_send.at[index],
            recv_sem=anchor_recv.at[g],
            device_id=(grp, w),
            device_id_type=MESH,
        )

    for j in range(1, chips):
        anchor_copy(((chip + j) % chips) * 2 + core, j).start()
    anchor_copy(sibling, 0).start()

    def query_source(i):
        s = i // n_grp
        head = i % n_grp
        return query_hbm.at[
            pl.ds(pl.multiple_of(s * slab, 16), slab), pl.ds(pl.multiple_of(head * cols, LANES), cols)
        ]

    def query_copy(i):
        return pltpu.make_async_remote_copy(
            src_ref=query_source(i),
            dst_ref=region_query.at[w],
            send_sem=query_send.at[i],
            recv_sem=query_recv.at[w],
            device_id=(i % n_grp, g * slabs + i // n_grp),
            device_id_type=MESH,
        )

    def is_self(i):
        return jnp.logical_and(g * slabs + i // n_grp == w, i % n_grp == g)

    @pl.loop(0, n_wide)
    def _(i):
        @pl.when(is_self(i))
        def _():
            pltpu.make_async_copy(query_source(i), region_query.at[w], query_recv.at[w]).start()

        @pl.when(jnp.logical_not(is_self(i)))
        def _():
            query_copy(i).start()

    low = lax.broadcasted_iota(jnp.int32, (BLK, LANES), 1) < HD

    def project(cell):
        both = jnp.dot(anchors[cell], weights[...], preferred_element_type=jnp.float32)
        rows = pl.ds(pl.multiple_of(cell * BLK, BLK), BLK)
        for j in range(pairs):
            k = both[:, j * LANES : (j + 1) * LANES]
            keys[j, 0, rows, :] = jnp.where(low, k, 0.0).astype(jnp.bfloat16)
            keys[j, 1, rows, :] = jnp.where(low, 0.0, k).astype(jnp.bfloat16)
        turned = both[:, cols:].T.astype(jnp.bfloat16)
        for h in range(2 * pairs):
            values[h, :HD, rows] = turned[h * HD : (h + 1) * HD]

    def wait_anchor(cell):
        pltpu.make_async_copy(anchors.at[cell], anchors.at[cell], anchor_recv.at[cell]).wait()

    def forward_copy(cell, j):
        return pltpu.make_async_remote_copy(
            src_ref=anchors.at[cell],
            dst_ref=anchors.at[cell],
            send_sem=forward_send.at[j],
            recv_sem=anchor_recv.at[cell],
            device_id=(sibling, w),
            device_id_type=MESH,
        )

    def across(j):
        return (chip + chips - j) % chips

    values[:, HD:, :] = jnp.ones((2 * pairs, ONES, values.shape[2]), jnp.bfloat16)
    for load in loads[:3]:
        load.wait()
    project(g)
    wait_anchor(sibling)
    project(sibling)
    for j in range(1, chips):
        cell = across(j) * 2 + core
        wait_anchor(cell)
        forward_copy(cell, j).start()
        project(cell)
    for j in range(1, chips):
        cell = across(j) * 2 + 1 - core
        wait_anchor(cell)
        project(cell)

    scale = math.log2(math.e) / math.sqrt(HD)
    group = STEP // slab
    blocks = STEP // BLK
    nt = (((1,), (1,)), ((), ()))

    def out_copy(p):
        return pltpu.make_async_remote_copy(
            src_ref=outgoing.at[p],
            dst_ref=attended.at[g, w % slabs],
            send_sem=out_send.at[p],
            recv_sem=out_recv.at[g, w % slabs],
            device_id=(home, p),
            device_id_type=MESH,
        )

    def listed(block):
        used = count_ref[block]
        bias = []
        for c in range(n_grp):
            live = jnp.logical_and(list_ref[0, block] == c, used > 0)
            for slot in range(1, LMAX):
                live = jnp.logical_or(live, jnp.logical_and(list_ref[slot, block] == c, used > slot))
            bias.append(jnp.full((1, BLK), jnp.where(live, 0.0, -jnp.inf), jnp.float32))
        return bias

    def attend(a):
        base = a * group
        biases = [listed(a * blocks + i) for i in range(blocks)]
        bias = [jnp.concatenate([one[c] for one in biases], axis=1) for c in range(n_grp)]
        for m in range(group):
            p = base + m
            pltpu.make_async_copy(region_query.at[p], region_query.at[p], query_recv.at[p]).wait()
        queries = region_query[pl.ds(base, group)].reshape(STEP, cols)
        heads = []
        for j in range(pairs):
            q = queries[:, j * LANES : (j + 1) * LANES]
            for i in range(2):
                scores = lax.dot_general(keys[j, i], q, nt, preferred_element_type=jnp.float32)
                cells = [scores[c * BLK : (c + 1) * BLK] for c in range(n_grp)]
                top = None
                for c in range(n_grp):
                    one = jnp.max(cells[c], axis=0, keepdims=True) * scale + bias[c]
                    top = one if top is None else jnp.maximum(top, one)
                expo = jnp.concatenate(
                    [
                        jnp.exp2(cells[c] * scale + (bias[c] - top)).astype(jnp.bfloat16)
                        for c in range(n_grp)
                    ],
                    axis=0,
                )
                summed = jnp.dot(values[2 * j + i], expo, preferred_element_type=jnp.float32)
                heads.append(summed[:HD] * (1.0 / summed[HD : HD + 1]))
        joined = jnp.concatenate(heads, axis=0).T.astype(jnp.bfloat16)
        outgoing[pl.ds(base, group)] = joined.reshape(group, slab, cols)
        for m in range(group):
            p = base + m
            mine = jnp.logical_and(p == w, here)

            @pl.when(mine)
            def _():
                pltpu.make_async_copy(
                    outgoing.at[p], attended.at[g, w % slabs], out_recv.at[g, w % slabs]
                ).start()

            @pl.when(jnp.logical_not(mine))
            def _():
                out_copy(p).start()

    groups = n_wide // group

    @pl.loop(0, groups)
    def _(t):
        k = (groups - t) % groups
        a = w // group
        bit = 1
        while bit < groups:
            a = a + ((k // bit) % 2) * bit * (1 - 2 * ((a // bit) % 2))
            bit *= 2
        attend(a)

    for load in loads[3:]:
        load.wait()
    for h in range(n_grp):
        for s in range(slabs):
            pltpu.make_async_copy(
                attended.at[h, s], attended.at[h, s], out_recv.at[h, s]
            ).wait()
    rows = query.shape[0]
    dim = query.shape[1]
    stream = []
    square = jnp.zeros((rows, 1), jnp.float32)
    for h in range(n_grp):
        part = query[:, h * cols : (h + 1) * cols].astype(jnp.float32) + attended[h].reshape(
            rows, cols
        ).astype(jnp.float32)
        square = square + jnp.sum(part * part, axis=-1, keepdims=True)
        stream.append(part)
    factor = lax.rsqrt(square / dim + 1e-06)
    normed = jnp.concatenate(
        [
            (stream[h] * factor * gain_ref[:, h * cols : (h + 1) * cols]).astype(jnp.bfloat16)
            for h in range(n_grp)
        ],
        axis=1,
    )
    hidden = jax.nn.gelu(
        jnp.dot(normed, up[...], preferred_element_type=jnp.float32), approximate=True
    ).astype(jnp.bfloat16)
    flux_ref[...] = lax.dot_general(flux_w_ref[...], hidden, nt, preferred_element_type=jnp.float32)

    for j in range(1, chips):
        anchor_copy(((chip + j) % chips) * 2 + core, j).wait_send()
        forward_copy(across(j) * 2 + core, j).wait_send()
    anchor_copy(sibling, 0).wait_send()

    @pl.loop(0, n_wide)
    def _(i):
        @pl.when(jnp.logical_not(is_self(i)))
        def _():
            query_copy(i).wait_send()

        @pl.when(jnp.logical_not(jnp.logical_and(i == w, here)))
        def _():
            out_copy(i).wait_send()


def body(n_wide, n_grp, anchor, key_w, value_w, query, cell_list, cell_count, gain, up, flux_w):
    rows, dim = query.shape
    cols = key_w.shape[1]
    slabs = n_wide // n_grp
    slab = rows // slabs
    cells = n_grp
    pairs = cols // LANES
    any_space = pl.BlockSpec(memory_space=pl.ANY)
    vmem = pl.BlockSpec(memory_space=pltpu.VMEM)
    smem = pl.BlockSpec(memory_space=pltpu.SMEM)
    bf16 = jnp.bfloat16
    dma = pltpu.SemaphoreType.DMA
    return pl.pallas_call(
        functools.partial(kernel, n_wide, n_grp),
        out_shape=jax.ShapeDtypeStruct((flux_w.shape[0], rows), jnp.float32),
        in_specs=[any_space] * 4 + [smem] * 2 + [vmem, any_space, vmem],
        out_specs=vmem,
        scratch_shapes=[
            pltpu.VMEM((cells, BLK, dim), bf16),
            pltpu.VMEM((dim, 2 * cols), bf16),
            pltpu.VMEM((pairs, 2, cells * BLK, LANES), bf16),
            pltpu.VMEM((2 * pairs, HD + ONES, cells * BLK), bf16),
            pltpu.VMEM((n_wide, slab, cols), bf16),
            pltpu.VMEM((n_wide, slab, cols), bf16),
            pltpu.VMEM((n_grp, slabs, slab, cols), bf16),
            pltpu.VMEM((rows, dim), bf16),
            pltpu.VMEM(up.shape, bf16),
            dma((5,)),
            dma((max(n_grp // 2, 1),)),
            dma((n_grp,)),
            dma((max(n_grp // 2, 1),)),
            dma((n_wide,)),
            dma((n_wide,)),
            dma((n_wide,)),
            dma((n_grp, slabs)),
        ],
        compiler_params=pltpu.CompilerParams(
            collective_id=0, has_side_effects=True, vmem_limit_bytes=56 * 1024 * 1024
        ),
        cost_estimate=pl.CostEstimate(flops=3 * 10**9, bytes_accessed=6 * 10**6, transcendentals=0),
    )(anchor, key_w, value_w, query, cell_list.T, cell_count, gain[None, :], up, flux_w)


def solution(mesh):
    in_specs = (
        P(("wide", "grp"), None),
        P(None, "grp"),
        P(None, "grp"),
        P(("wide", "grp"), None),
        P("wide", None),
        P("wide"),
        P(),
        P(),
        P(),
    )
    out_specs = P(None, ("wide", "grp"))
    step = functools.partial(body, mesh.shape["wide"], mesh.shape["grp"])
    return jax.shard_map(step, mesh=mesh, in_specs=in_specs, out_specs=out_specs, check_vma=False)
```

```python
import functools
import math

import jax
import jax.numpy as jnp
from jax import lax
from jax.experimental import pallas as pl
from jax.experimental.pallas import tpu as pltpu
from jax.sharding import PartitionSpec as P

BLK = 128
LMAX = 4
HD = 64
LANES = 128
ONES = 16
STEP = 256
MESH = pl.DeviceIdType.MESH


def kernel(
    n_wide,
    n_grp,
    anchor_hbm,
    key_hbm,
    value_hbm,
    query_hbm,
    list_ref,
    count_ref,
    gain_ref,
    up_hbm,
    flux_w_ref,
    flux_ref,
    anchors,
    weights,
    keys,
    values,
    region_query,
    outgoing,
    attended,
    query,
    up,
    back,
    local_sem,
    anchor_send,
    anchor_recv,
    forward_send,
    query_send,
    query_recv,
    out_send,
    out_recv,
    back_send,
    back_recv,
):
    w = lax.axis_index("wide")
    g = lax.axis_index("grp")
    slabs = n_wide // n_grp
    slab = region_query.shape[1]
    cols = region_query.shape[2]
    pairs = cols // LANES
    chips = n_grp // 2
    core = g % 2
    chip = g // 2
    sibling = chip * 2 + 1 - core
    home = w // slabs
    here = home == g

    loads = [
        pltpu.make_async_copy(anchor_hbm, anchors.at[g], local_sem.at[0]),
        pltpu.make_async_copy(key_hbm, weights.at[:, pl.ds(0, cols)], local_sem.at[1]),
        pltpu.make_async_copy(value_hbm, weights.at[:, pl.ds(cols, cols)], local_sem.at[2]),
        pltpu.make_async_copy(query_hbm, query, local_sem.at[3]),
        pltpu.make_async_copy(up_hbm, up, local_sem.at[4]),
    ]
    for load in loads:
        load.start()

    barrier = pltpu.get_barrier_semaphore()

    def greet(wide, grp):
        pl.semaphore_signal(barrier, inc=1, device_id=(grp, wide), device_id_type=MESH)

    @pl.loop(1, n_grp)
    def _(i):
        greet(w, (g + i) % n_grp)

    @pl.loop(0, n_wide)
    def _(i):
        region = g * slabs + i // n_grp
        head = i % n_grp

        @pl.when(jnp.logical_or(region != w, head != g))
        def _():
            greet(region, head)

        @pl.when(jnp.logical_or(i != w, home != g))
        def _():
            greet(i, home)

    @pl.loop(1, n_wide)
    def _(i):
        greet((w + i) % n_wide, g)

    pl.semaphore_wait(barrier, n_grp - 2 + 3 * n_wide - 2 * here.astype(jnp.int32))

    def anchor_copy(grp, index):
        return pltpu.make_async_remote_copy(
            src_ref=anchor_hbm,
            dst_ref=anchors.at[g],
            send_sem=anchor_send.at[index],
            recv_sem=anchor_recv.at[g],
            device_id=(grp, w),
            device_id_type=MESH,
        )

    for j in range(1, chips):
        anchor_copy(((chip + j) % chips) * 2 + core, j).start()
    anchor_copy(sibling, 0).start()

    def query_source(i):
        s = i // n_grp
        head = i % n_grp
        return query_hbm.at[
            pl.ds(pl.multiple_of(s * slab, 16), slab), pl.ds(pl.multiple_of(head * cols, LANES), cols)
        ]

    def query_copy(i):
        return pltpu.make_async_remote_copy(
            src_ref=query_source(i),
            dst_ref=region_query.at[w],
            send_sem=query_send.at[i],
            recv_sem=query_recv.at[w],
            device_id=(i % n_grp, g * slabs + i // n_grp),
            device_id_type=MESH,
        )

    def is_self(i):
        return jnp.logical_and(g * slabs + i // n_grp == w, i % n_grp == g)

    def send_queries(near):
        @pl.loop(0, n_wide)
        def _(i):
            chosen = ((i % n_grp) // 2 == chip) if near else ((i % n_grp) // 2 != chip)

            if near:

                @pl.when(is_self(i))
                def _():
                    pltpu.make_async_copy(
                        query_source(i), region_query.at[w], query_recv.at[w]
                    ).start()

            @pl.when(jnp.logical_and(chosen, jnp.logical_not(is_self(i))))
            def _():
                query_copy(i).start()

    send_queries(True)

    low = lax.broadcasted_iota(jnp.int32, (BLK, LANES), 1) < HD

    def project(cell):
        both = jnp.dot(anchors[cell], weights[...], preferred_element_type=jnp.float32)
        rows = pl.ds(pl.multiple_of(cell * BLK, BLK), BLK)
        for j in range(pairs):
            k = both[:, j * LANES : (j + 1) * LANES]
            keys[j, 0, rows, :] = jnp.where(low, k, 0.0).astype(jnp.bfloat16)
            keys[j, 1, rows, :] = jnp.where(low, 0.0, k).astype(jnp.bfloat16)
        turned = both[:, cols:].T.astype(jnp.bfloat16)
        for h in range(2 * pairs):
            values[h, :HD, rows] = turned[h * HD : (h + 1) * HD]

    def wait_anchor(cell):
        pltpu.make_async_copy(anchors.at[cell], anchors.at[cell], anchor_recv.at[cell]).wait()

    def forward_copy(cell, j):
        return pltpu.make_async_remote_copy(
            src_ref=anchors.at[cell],
            dst_ref=anchors.at[cell],
            send_sem=forward_send.at[j],
            recv_sem=anchor_recv.at[cell],
            device_id=(sibling, w),
            device_id_type=MESH,
        )

    def across(j):
        return (chip + chips - j) % chips

    values[:, HD:, :] = jnp.ones((2 * pairs, ONES, values.shape[2]), jnp.bfloat16)
    for load in loads[:3]:
        load.wait()
    project(g)
    wait_anchor(sibling)
    project(sibling)
    for j in range(1, chips):
        cell = across(j) * 2 + core
        wait_anchor(cell)
        forward_copy(cell, j).start()
    send_queries(False)
    for j in range(1, chips):
        project(across(j) * 2 + core)
    for j in range(1, chips):
        cell = across(j) * 2 + 1 - core
        wait_anchor(cell)
        project(cell)

    scale = math.log2(math.e) / math.sqrt(HD)
    group = STEP // slab
    blocks = STEP // BLK
    nt = (((1,), (1,)), ((), ()))

    def out_copy(p):
        return pltpu.make_async_remote_copy(
            src_ref=outgoing.at[p],
            dst_ref=attended.at[g, w % slabs],
            send_sem=out_send.at[p],
            recv_sem=out_recv.at[g, w % slabs],
            device_id=(home, p),
            device_id_type=MESH,
        )

    half = n_wide // 2

    def far(p):
        return p // half != w // half

    def hops(p):
        return jnp.logical_and(far(p), home // 2 != chip)

    def hop_copy(p):
        return pltpu.make_async_remote_copy(
            src_ref=outgoing.at[p],
            dst_ref=back.at[w],
            send_sem=out_send.at[p],
            recv_sem=back_recv.at[w],
            device_id=(g, p),
            device_id_type=MESH,
        )

    def back_copy(r):
        return pltpu.make_async_remote_copy(
            src_ref=back.at[r],
            dst_ref=attended.at[g, r % slabs],
            send_sem=back_send.at[r],
            recv_sem=out_recv.at[g, r % slabs],
            device_id=(r // slabs, w),
            device_id_type=MESH,
        )

    def passed_on(r):
        return jnp.logical_and(far(r), (r // slabs) // 2 != chip)

    def flipped(index, k, count):
        bit = 1
        while bit < count:
            index = index + ((k // bit) % 2) * bit * (1 - 2 * ((index // bit) % 2))
            bit *= 2
        return index

    def listed(block):
        used = count_ref[block]
        bias = []
        for c in range(n_grp):
            live = jnp.logical_and(list_ref[0, block] == c, used > 0)
            for slot in range(1, LMAX):
                live = jnp.logical_or(live, jnp.logical_and(list_ref[slot, block] == c, used > slot))
            bias.append(jnp.full((1, BLK), jnp.where(live, 0.0, -jnp.inf), jnp.float32))
        return bias

    def attend(a):
        base = a * group
        biases = [listed(a * blocks + i) for i in range(blocks)]
        bias = [jnp.concatenate([one[c] for one in biases], axis=1) for c in range(n_grp)]
        for m in range(group):
            p = base + m
            pltpu.make_async_copy(region_query.at[p], region_query.at[p], query_recv.at[p]).wait()
        queries = region_query[pl.ds(base, group)].reshape(STEP, cols)
        heads = []
        for j in range(pairs):
            q = queries[:, j * LANES : (j + 1) * LANES]
            for i in range(2):
                scores = lax.dot_general(keys[j, i], q, nt, preferred_element_type=jnp.float32)
                cells = [scores[c * BLK : (c + 1) * BLK] for c in range(n_grp)]
                top = None
                for c in range(n_grp):
                    one = jnp.max(cells[c], axis=0, keepdims=True) * scale + bias[c]
                    top = one if top is None else jnp.maximum(top, one)
                expo = jnp.concatenate(
                    [
                        jnp.exp2(cells[c] * scale + (bias[c] - top)).astype(jnp.bfloat16)
                        for c in range(n_grp)
                    ],
                    axis=0,
                )
                summed = jnp.dot(values[2 * j + i], expo, preferred_element_type=jnp.float32)
                heads.append(summed[:HD] * (1.0 / summed[HD : HD + 1]))
        joined = jnp.concatenate(heads, axis=0).T.astype(jnp.bfloat16)
        outgoing[pl.ds(base, group)] = joined.reshape(group, slab, cols)
        for m in range(group):
            p = base + m
            mine = jnp.logical_and(p == w, here)

            @pl.when(mine)
            def _():
                pltpu.make_async_copy(
                    outgoing.at[p], attended.at[g, w % slabs], out_recv.at[g, w % slabs]
                ).start()

            @pl.when(hops(p))
            def _():
                hop_copy(p).start()

            @pl.when(jnp.logical_not(jnp.logical_or(mine, hops(p))))
            def _():
                out_copy(p).start()

    groups = n_wide // group

    @pl.loop(0, groups)
    def _(t):
        attend(flipped(w // group, t, groups))

    @pl.loop(half, n_wide)
    def _(k):
        r = flipped(w, k, n_wide)

        @pl.when(passed_on(r))
        def _():
            pltpu.make_async_copy(back.at[r], back.at[r], back_recv.at[r]).wait()
            back_copy(r).start()

    for load in loads[3:]:
        load.wait()
    for h in range(n_grp):
        for s in range(slabs):
            pltpu.make_async_copy(
                attended.at[h, s], attended.at[h, s], out_recv.at[h, s]
            ).wait()
    rows = query.shape[0]
    dim = query.shape[1]
    stream = []
    square = jnp.zeros((rows, 1), jnp.float32)
    for h in range(n_grp):
        part = query[:, h * cols : (h + 1) * cols].astype(jnp.float32) + attended[h].reshape(
            rows, cols
        ).astype(jnp.float32)
        square = square + jnp.sum(part * part, axis=-1, keepdims=True)
        stream.append(part)
    factor = lax.rsqrt(square / dim + 1e-06)
    normed = jnp.concatenate(
        [
            (stream[h] * factor * gain_ref[:, h * cols : (h + 1) * cols]).astype(jnp.bfloat16)
            for h in range(n_grp)
        ],
        axis=1,
    )
    hidden = jax.nn.gelu(
        jnp.dot(normed, up[...], preferred_element_type=jnp.float32), approximate=True
    ).astype(jnp.bfloat16)
    flux_ref[...] = lax.dot_general(flux_w_ref[...], hidden, nt, preferred_element_type=jnp.float32)

    for j in range(1, chips):
        anchor_copy(((chip + j) % chips) * 2 + core, j).wait_send()
        forward_copy(across(j) * 2 + core, j).wait_send()
    anchor_copy(sibling, 0).wait_send()

    @pl.loop(0, n_wide)
    def _(i):
        @pl.when(jnp.logical_not(is_self(i)))
        def _():
            query_copy(i).wait_send()

        @pl.when(jnp.logical_not(jnp.logical_and(i == w, here)))
        def _():
            out_copy(i).wait_send()

        @pl.when(passed_on(i))
        def _():
            back_copy(i).wait_send()


def body(n_wide, n_grp, anchor, key_w, value_w, query, cell_list, cell_count, gain, up, flux_w):
    rows, dim = query.shape
    cols = key_w.shape[1]
    slabs = n_wide // n_grp
    slab = rows // slabs
    cells = n_grp
    pairs = cols // LANES
    any_space = pl.BlockSpec(memory_space=pl.ANY)
    vmem = pl.BlockSpec(memory_space=pltpu.VMEM)
    smem = pl.BlockSpec(memory_space=pltpu.SMEM)
    bf16 = jnp.bfloat16
    dma = pltpu.SemaphoreType.DMA
    return pl.pallas_call(
        functools.partial(kernel, n_wide, n_grp),
        out_shape=jax.ShapeDtypeStruct((flux_w.shape[0], rows), jnp.float32),
        in_specs=[any_space] * 4 + [smem] * 2 + [vmem, any_space, vmem],
        out_specs=vmem,
        scratch_shapes=[
            pltpu.VMEM((cells, BLK, dim), bf16),
            pltpu.VMEM((dim, 2 * cols), bf16),
            pltpu.VMEM((pairs, 2, cells * BLK, LANES), bf16),
            pltpu.VMEM((2 * pairs, HD + ONES, cells * BLK), bf16),
            pltpu.VMEM((n_wide, slab, cols), bf16),
            pltpu.VMEM((n_wide, slab, cols), bf16),
            pltpu.VMEM((n_grp, slabs, slab, cols), bf16),
            pltpu.VMEM((rows, dim), bf16),
            pltpu.VMEM(up.shape, bf16),
            pltpu.VMEM((n_wide, slab, cols), bf16),
            dma((5,)),
            dma((max(n_grp // 2, 1),)),
            dma((n_grp,)),
            dma((max(n_grp // 2, 1),)),
            dma((n_wide,)),
            dma((n_wide,)),
            dma((n_wide,)),
            dma((n_grp, slabs)),
            dma((n_wide,)),
            dma((n_wide,)),
        ],
        compiler_params=pltpu.CompilerParams(
            collective_id=0, has_side_effects=True, vmem_limit_bytes=56 * 1024 * 1024
        ),
        cost_estimate=pl.CostEstimate(flops=3 * 10**9, bytes_accessed=6 * 10**6, transcendentals=0),
    )(anchor, key_w, value_w, query, cell_list.T, cell_count, gain[None, :], up, flux_w)


def solution(mesh):
    in_specs = (
        P(("wide", "grp"), None),
        P(None, "grp"),
        P(None, "grp"),
        P(("wide", "grp"), None),
        P("wide", None),
        P("wide"),
        P(),
        P(),
        P(),
    )
    out_specs = P(None, ("wide", "grp"))
    step = functools.partial(body, mesh.shape["wide"], mesh.shape["grp"])
    return jax.shard_map(step, mesh=mesh, in_specs=in_specs, out_specs=out_specs, check_vma=False)
```

```python
import functools
import math

import jax
import jax.numpy as jnp
from jax import lax
from jax.experimental import pallas as pl
from jax.experimental.pallas import tpu as pltpu
from jax.sharding import PartitionSpec as P

BLK = 128
LMAX = 4
HD = 64
LANES = 128
ONES = 16
STEP = 256
MESH = pl.DeviceIdType.MESH


def kernel(
    n_wide,
    n_grp,
    anchor_hbm,
    key_hbm,
    value_hbm,
    query_hbm,
    list_ref,
    count_ref,
    gain_ref,
    up_hbm,
    flux_w_ref,
    flux_ref,
    anchors,
    weights,
    keys,
    values,
    region_query,
    outgoing,
    attended,
    query,
    up,
    back,
    local_sem,
    anchor_send,
    anchor_recv,
    forward_send,
    query_send,
    query_recv,
    out_send,
    out_recv,
    back_send,
    back_recv,
):
    w = lax.axis_index("wide")
    g = lax.axis_index("grp")
    slabs = n_wide // n_grp
    slab = region_query.shape[1]
    cols = region_query.shape[2]
    pairs = cols // LANES
    chips = n_grp // 2
    core = g % 2
    chip = g // 2
    sibling = chip * 2 + 1 - core
    home = w // slabs
    here = home == g

    loads = [
        pltpu.make_async_copy(anchor_hbm, anchors.at[g], local_sem.at[0]),
        pltpu.make_async_copy(key_hbm, weights.at[:, pl.ds(0, cols)], local_sem.at[1]),
        pltpu.make_async_copy(value_hbm, weights.at[:, pl.ds(cols, cols)], local_sem.at[2]),
        pltpu.make_async_copy(query_hbm, query, local_sem.at[3]),
        pltpu.make_async_copy(up_hbm, up, local_sem.at[4]),
    ]
    for load in loads:
        load.start()

    barrier = pltpu.get_barrier_semaphore()

    def greet(wide, grp):
        pl.semaphore_signal(barrier, inc=1, device_id=(grp, wide), device_id_type=MESH)

    @pl.loop(1, n_grp)
    def _(i):
        greet(w, (g + i) % n_grp)

    @pl.loop(0, n_wide)
    def _(i):
        region = g * slabs + i // n_grp
        head = i % n_grp

        @pl.when(jnp.logical_or(region != w, head != g))
        def _():
            greet(region, head)

        @pl.when(jnp.logical_or(i != w, home != g))
        def _():
            greet(i, home)

    @pl.loop(1, n_wide)
    def _(i):
        greet((w + i) % n_wide, g)

    pl.semaphore_wait(barrier, n_grp - 2 + 3 * n_wide - 2 * here.astype(jnp.int32))

    def anchor_copy(grp, index):
        return pltpu.make_async_remote_copy(
            src_ref=anchor_hbm,
            dst_ref=anchors.at[g],
            send_sem=anchor_send.at[index],
            recv_sem=anchor_recv.at[g],
            device_id=(grp, w),
            device_id_type=MESH,
        )

    for j in range(1, chips):
        anchor_copy(((chip + j) % chips) * 2 + core, j).start()
    anchor_copy(sibling, 0).start()

    def query_source(i):
        s = i // n_grp
        head = i % n_grp
        return query_hbm.at[
            pl.ds(pl.multiple_of(s * slab, 16), slab), pl.ds(pl.multiple_of(head * cols, LANES), cols)
        ]

    def query_copy(i):
        return pltpu.make_async_remote_copy(
            src_ref=query_source(i),
            dst_ref=region_query.at[w],
            send_sem=query_send.at[i],
            recv_sem=query_recv.at[w],
            device_id=(i % n_grp, g * slabs + i // n_grp),
            device_id_type=MESH,
        )

    def is_self(i):
        return jnp.logical_and(g * slabs + i // n_grp == w, i % n_grp == g)

    @pl.loop(0, n_wide)
    def _(i):
        @pl.when(is_self(i))
        def _():
            pltpu.make_async_copy(query_source(i), region_query.at[w], query_recv.at[w]).start()

        @pl.when(jnp.logical_not(is_self(i)))
        def _():
            query_copy(i).start()

    low = lax.broadcasted_iota(jnp.int32, (BLK, LANES), 1) < HD

    def project(cell):
        both = jnp.dot(anchors[cell], weights[...], preferred_element_type=jnp.float32)
        rows = pl.ds(pl.multiple_of(cell * BLK, BLK), BLK)
        for j in range(pairs):
            k = both[:, j * LANES : (j + 1) * LANES]
            keys[j, 0, rows, :] = jnp.where(low, k, 0.0).astype(jnp.bfloat16)
            keys[j, 1, rows, :] = jnp.where(low, 0.0, k).astype(jnp.bfloat16)
        turned = both[:, cols:].T.astype(jnp.bfloat16)
        for h in range(2 * pairs):
            values[h, :HD, rows] = turned[h * HD : (h + 1) * HD]

    def wait_anchor(cell):
        pltpu.make_async_copy(anchors.at[cell], anchors.at[cell], anchor_recv.at[cell]).wait()

    def forward_copy(cell, j):
        return pltpu.make_async_remote_copy(
            src_ref=anchors.at[cell],
            dst_ref=anchors.at[cell],
            send_sem=forward_send.at[j],
            recv_sem=anchor_recv.at[cell],
            device_id=(sibling, w),
            device_id_type=MESH,
        )

    def across(j):
        return (chip + chips - j) % chips

    values[:, HD:, :] = jnp.ones((2 * pairs, ONES, values.shape[2]), jnp.bfloat16)
    for load in loads[:3]:
        load.wait()
    project(g)
    wait_anchor(sibling)
    project(sibling)
    for j in range(1, chips):
        cell = across(j) * 2 + core
        wait_anchor(cell)
        forward_copy(cell, j).start()
    for j in range(1, chips):
        project(across(j) * 2 + core)
    for j in range(1, chips):
        cell = across(j) * 2 + 1 - core
        wait_anchor(cell)
        project(cell)

    scale = math.log2(math.e) / math.sqrt(HD)
    group = STEP // slab
    blocks = STEP // BLK
    nt = (((1,), (1,)), ((), ()))

    def out_copy(p):
        return pltpu.make_async_remote_copy(
            src_ref=outgoing.at[p],
            dst_ref=attended.at[g, w % slabs],
            send_sem=out_send.at[p],
            recv_sem=out_recv.at[g, w % slabs],
            device_id=(home, p),
            device_id_type=MESH,
        )

    half = n_wide // 2

    def far(p):
        return p // half != w // half

    def hops(p):
        return jnp.logical_and(far(p), home // 2 != chip)

    def hop_copy(p):
        return pltpu.make_async_remote_copy(
            src_ref=outgoing.at[p],
            dst_ref=back.at[w],
            send_sem=out_send.at[p],
            recv_sem=back_recv.at[w],
            device_id=(g, p),
            device_id_type=MESH,
        )

    def back_copy(r):
        return pltpu.make_async_remote_copy(
            src_ref=back.at[r],
            dst_ref=attended.at[g, r % slabs],
            send_sem=back_send.at[r],
            recv_sem=out_recv.at[g, r % slabs],
            device_id=(r // slabs, w),
            device_id_type=MESH,
        )

    def passed_on(r):
        return jnp.logical_and(far(r), (r // slabs) // 2 != chip)

    def flipped(index, k, count):
        bit = 1
        while bit < count:
            index = index + ((k // bit) % 2) * bit * (1 - 2 * ((index // bit) % 2))
            bit *= 2
        return index

    def listed(block):
        used = count_ref[block]
        bias = []
        for c in range(n_grp):
            live = jnp.logical_and(list_ref[0, block] == c, used > 0)
            for slot in range(1, LMAX):
                live = jnp.logical_or(live, jnp.logical_and(list_ref[slot, block] == c, used > slot))
            bias.append(jnp.full((1, BLK), jnp.where(live, 0.0, -jnp.inf), jnp.float32))
        return bias

    def attend(a):
        base = a * group
        biases = [listed(a * blocks + i) for i in range(blocks)]
        bias = [jnp.concatenate([one[c] for one in biases], axis=1) for c in range(n_grp)]
        for m in range(group):
            p = base + m
            pltpu.make_async_copy(region_query.at[p], region_query.at[p], query_recv.at[p]).wait()
        queries = region_query[pl.ds(base, group)].reshape(STEP, cols)
        heads = []
        for j in range(pairs):
            q = queries[:, j * LANES : (j + 1) * LANES]
            for i in range(2):
                scores = lax.dot_general(keys[j, i], q, nt, preferred_element_type=jnp.float32)
                cells = [scores[c * BLK : (c + 1) * BLK] for c in range(n_grp)]
                top = None
                for c in range(n_grp):
                    one = jnp.max(cells[c], axis=0, keepdims=True) * scale + bias[c]
                    top = one if top is None else jnp.maximum(top, one)
                expo = jnp.concatenate(
                    [
                        jnp.exp2(cells[c] * scale + (bias[c] - top)).astype(jnp.bfloat16)
                        for c in range(n_grp)
                    ],
                    axis=0,
                )
                summed = jnp.dot(values[2 * j + i], expo, preferred_element_type=jnp.float32)
                heads.append(summed[:HD] * (1.0 / summed[HD : HD + 1]))
        joined = jnp.concatenate(heads, axis=0).T.astype(jnp.bfloat16)
        outgoing[pl.ds(base, group)] = joined.reshape(group, slab, cols)
        for m in range(group):
            p = base + m
            mine = jnp.logical_and(p == w, here)

            @pl.when(mine)
            def _():
                pltpu.make_async_copy(
                    outgoing.at[p], attended.at[g, w % slabs], out_recv.at[g, w % slabs]
                ).start()

            @pl.when(hops(p))
            def _():
                hop_copy(p).start()

            @pl.when(jnp.logical_not(jnp.logical_or(mine, hops(p))))
            def _():
                out_copy(p).start()

    groups = n_wide // group

    @pl.loop(0, groups)
    def _(t):
        attend(flipped(w // group, t, groups))

    @pl.loop(half, n_wide)
    def _(k):
        r = flipped(w, k, n_wide)

        @pl.when(passed_on(r))
        def _():
            pltpu.make_async_copy(back.at[r], back.at[r], back_recv.at[r]).wait()
            back_copy(r).start()

    for load in loads[3:]:
        load.wait()
    for h in range(n_grp):
        for s in range(slabs):
            pltpu.make_async_copy(
                attended.at[h, s], attended.at[h, s], out_recv.at[h, s]
            ).wait()
    rows = query.shape[0]
    dim = query.shape[1]
    stream = []
    square = jnp.zeros((rows, 1), jnp.float32)
    for h in range(n_grp):
        part = query[:, h * cols : (h + 1) * cols].astype(jnp.float32) + attended[h].reshape(
            rows, cols
        ).astype(jnp.float32)
        square = square + jnp.sum(part * part, axis=-1, keepdims=True)
        stream.append(part)
    factor = lax.rsqrt(square / dim + 1e-06)
    normed = jnp.concatenate(
        [
            (stream[h] * factor * gain_ref[:, h * cols : (h + 1) * cols]).astype(jnp.bfloat16)
            for h in range(n_grp)
        ],
        axis=1,
    )
    hidden = jax.nn.gelu(
        jnp.dot(normed, up[...], preferred_element_type=jnp.float32), approximate=True
    ).astype(jnp.bfloat16)
    flux_ref[...] = lax.dot_general(flux_w_ref[...], hidden, nt, preferred_element_type=jnp.float32)

    for j in range(1, chips):
        anchor_copy(((chip + j) % chips) * 2 + core, j).wait_send()
        forward_copy(across(j) * 2 + core, j).wait_send()
    anchor_copy(sibling, 0).wait_send()

    @pl.loop(0, n_wide)
    def _(i):
        @pl.when(jnp.logical_not(is_self(i)))
        def _():
            query_copy(i).wait_send()

        @pl.when(jnp.logical_not(jnp.logical_and(i == w, here)))
        def _():
            out_copy(i).wait_send()

        @pl.when(passed_on(i))
        def _():
            back_copy(i).wait_send()


def body(n_wide, n_grp, anchor, key_w, value_w, query, cell_list, cell_count, gain, up, flux_w):
    rows, dim = query.shape
    cols = key_w.shape[1]
    slabs = n_wide // n_grp
    slab = rows // slabs
    cells = n_grp
    pairs = cols // LANES
    any_space = pl.BlockSpec(memory_space=pl.ANY)
    vmem = pl.BlockSpec(memory_space=pltpu.VMEM)
    smem = pl.BlockSpec(memory_space=pltpu.SMEM)
    bf16 = jnp.bfloat16
    dma = pltpu.SemaphoreType.DMA
    return pl.pallas_call(
        functools.partial(kernel, n_wide, n_grp),
        out_shape=jax.ShapeDtypeStruct((flux_w.shape[0], rows), jnp.float32),
        in_specs=[any_space] * 4 + [smem] * 2 + [vmem, any_space, vmem],
        out_specs=vmem,
        scratch_shapes=[
            pltpu.VMEM((cells, BLK, dim), bf16),
            pltpu.VMEM((dim, 2 * cols), bf16),
            pltpu.VMEM((pairs, 2, cells * BLK, LANES), bf16),
            pltpu.VMEM((2 * pairs, HD + ONES, cells * BLK), bf16),
            pltpu.VMEM((n_wide, slab, cols), bf16),
            pltpu.VMEM((n_wide, slab, cols), bf16),
            pltpu.VMEM((n_grp, slabs, slab, cols), bf16),
            pltpu.VMEM((rows, dim), bf16),
            pltpu.VMEM(up.shape, bf16),
            pltpu.VMEM((n_wide, slab, cols), bf16),
            dma((5,)),
            dma((max(n_grp // 2, 1),)),
            dma((n_grp,)),
            dma((max(n_grp // 2, 1),)),
            dma((n_wide,)),
            dma((n_wide,)),
            dma((n_wide,)),
            dma((n_grp, slabs)),
            dma((n_wide,)),
            dma((n_wide,)),
        ],
        compiler_params=pltpu.CompilerParams(
            collective_id=0, has_side_effects=True, vmem_limit_bytes=56 * 1024 * 1024
        ),
        cost_estimate=pl.CostEstimate(flops=3 * 10**9, bytes_accessed=6 * 10**6, transcendentals=0),
    )(anchor, key_w, value_w, query, cell_list.T, cell_count, gain[None, :], up, flux_w)


def solution(mesh):
    in_specs = (
        P(("wide", "grp"), None),
        P(None, "grp"),
        P(None, "grp"),
        P(("wide", "grp"), None),
        P("wide", None),
        P("wide"),
        P(),
        P(),
        P(),
    )
    out_specs = P(None, ("wide", "grp"))
    step = functools.partial(body, mesh.shape["wide"], mesh.shape["grp"])
    return jax.shard_map(step, mesh=mesh, in_specs=in_specs, out_specs=out_specs, check_vma=False)
```
